256 devices in a mesh: wide: 32 (over x, z), narrow: 8 (over y, core).
Axes of the slice: x: 4, y: 4, z: 8, core: 2. Of those that a mesh axis runs over, the one named last changes fastest.
Arguments:
- panel_loads: float32 [2, 2048, 256], P(None, 'narrow'), may hold values from -6 to 6
- tail_loads: float32 [98304, 256], P(('narrow', 'wide')), may hold values from -6 to 6
- inverses: float32 [2, 2048, 2048], P(None, 'wide', 'narrow'), may hold values from -0.125 to 0.125
- cross_factor: float32 [2048, 2048], P('wide', 'narrow'), may hold values from -0.125 to 0.125
- tail_factor: float32 [2, 2048, 98304], P(None, 'wide', 'narrow'), may hold values from -0.1875 to 0.1875
Outputs:
- solution: float32 [2, 2048, 256], P(None, 'wide')
- tail_rest: float32 [98304, 256], P(('narrow', 'wide'))
The draws below stay inside these ranges and needn't reach their ends.
All inputs are finite; a program needn't handle non-finite values.
Results may differ from the reference program's by a relative error of at most 0.000082.
Values sent between devices are 32-bit elements; how exact they have to be, the bound alone decides.
A program may use at most 128 MiB of HBM per device.

```python
import jax
import jax.numpy as jnp
from jax import lax

W = 2048
R = 256
TAIL = 98304


def spiked(entries, stream_key, source, target, blocks, factor):
    owner, partner = [(jnp.arange(entries.shape[axis_at]) // (entries.shape[axis_at] // blocks)).reshape([-1 if axis == axis_at else 1 for axis in range(entries.ndim)]) for axis_at in (source, target)]
    chosen = jax.random.permutation(stream_key, blocks)[partner]
    strong = (owner == chosen) | (owner == (partner + blocks // 2) % blocks)
    return jnp.where(strong, factor * entries, entries)


def block_levels(key, dims, shards, least, high):
    def one(axis_at, shards_of):
        steps = jax.random.uniform(jax.random.fold_in(jax.random.fold_in(key, 6), axis_at), (shards_of,), jnp.float32, least / len(shards), high / len(shards))
        return jnp.repeat(jnp.exp(steps), dims[axis_at] // shards_of).reshape((-1,) + (1,) * (len(dims) - axis_at - 1))

    factor_of = one(*shards[0])
    for cut in shards[1:]:
        factor_of = factor_of * one(*cut)
    return factor_of


def centred(own_key, dims, deviation, bound, pieces=(), dtype=jnp.bfloat16):
    gain = block_levels(own_key, dims, pieces, -0.22, 0.18) if pieces else 1.0
    entries = jax.random.normal(own_key, dims, jnp.float32) * deviation * gain
    return jnp.minimum(jnp.maximum(entries, -bound), bound).astype(dtype)


def gaussian_with(rng, shape, width, limit, shards, heavy, dtype=jnp.bfloat16):
    values = width * jax.random.normal(rng, shape, jnp.float32)
    if shards:
        values = values * block_levels(rng, shape, shards, -0.22, 0.18)
    return jnp.clip(spiked(values, jax.random.fold_in(rng, 3), *heavy), -limit, limit).astype(dtype)


def setup_inputs(seed: int = 0) -> dict:
    streams_of = jax.random.split(jax.random.key(seed), 6)
    return {
        "panel_loads": centred(streams_of[0], (2, W, R), 1.0, 6.0, ((1, 8),), jnp.float32),
        "tail_loads": centred(streams_of[1], (TAIL, R), 1.0, 6.0, ((0, 256),), jnp.float32),
        "inverses": centred(streams_of[2], (2, W, W), W ** -0.5, 0.125, ((1, 32), (2, 8)), jnp.float32),
        "cross_factor": centred(streams_of[3], (W, W), W ** -0.5, 0.125, ((0, 32), (1, 8)), jnp.float32),
        "tail_factor": gaussian_with(streams_of[4], (2, W, TAIL), (2 * W) ** -0.5, 0.1875, ((1, 32), (2, 8)), (1, 2, 32, 2.75), jnp.float32),
    }


def reference(panel_loads, tail_loads, inverses, cross_factor, tail_factor):
    high = lax.Precision.HIGHEST
    first = jnp.dot(inverses[0], panel_loads[0], precision=high, preferred_element_type=jnp.float32)
    carried = lax.dot_general(cross_factor, first, (((0,), (0,)), ((), ())), precision=high, preferred_element_type=jnp.float32)
    rest = panel_loads[1] - carried
    second = jnp.dot(inverses[1], rest, precision=high, preferred_element_type=jnp.float32)
    solution = jnp.stack([first, second])
    update = lax.dot_general(tail_factor[0], first, (((0,), (0,)), ((), ())), precision=high, preferred_element_type=jnp.float32)
    update = update + lax.dot_general(tail_factor[1], second, (((0,), (0,)), ((), ())), precision=high, preferred_element_type=jnp.float32)
    return solution, tail_loads - update
```

```python
import functools

import jax
import jax.numpy as jnp
from jax import lax
from jax.experimental import pallas as pl
from jax.experimental.pallas import tpu as pltpu
from jax.sharding import PartitionSpec as P

MESH = pl.DeviceIdType.MESH
NX, NZ, NY = 4, 8, 4
NW = NX * NZ
ROWS = 384
R1 = 256
R2 = 128
HIGH = lax.Precision.HIGHEST
F32 = jnp.float32
BF16 = jnp.bfloat16


def dot(a, b):
    return jnp.dot(a, b, precision=HIGH, preferred_element_type=F32)


def split(a):
    hi = a.astype(BF16)
    return hi, (a - hi.astype(F32)).astype(BF16)


def dot3(xh, xl, a):
    ah, al = split(a)
    out = jnp.dot(xh, ah, preferred_element_type=F32)
    out += jnp.dot(xl, ah, preferred_element_type=F32)
    return out + jnp.dot(xh, al, preferred_element_type=F32)


def kernel(
    pl_ref, inv_ref, cross_ref, loads_ref, tail_ref,
    sol_ref, out_ref,
    part, corebuf, ybuf, xg, xz, cpart, crecv, restall,
    a1, a2, pb, qb, recv1, xr0, xr1, farsum, farrecv, xt,
    core_s, core_r, y_s, y_r, cg_s, cg_r, known,
    rs_s, rs_r, ag_s, ag_r, gx_s, gx_r, gz_s, gz_r,
    a1_s, a1_r, a1_l, a2_s, a2_r, a2_l,
    b1_s, b1_r, b2_s, b2_r, b3_s, b3_r,
):
    w = lax.axis_index("wide")
    n = lax.axis_index("narrow")
    x, z = w // NZ, w % NZ
    y, core = n // 2, n % 2

    def xpos(d):
        return (x + d + NX) % NX

    def zpos(d):
        return (z + d + NZ) % NZ

    def at_x(d):
        return (xpos(d) * NZ + z, n)

    def at_z(d):
        return (x * NZ + zpos(d), n)

    def at_y(d):
        return (w, ((y + d) % NY) * 2 + core)

    other = (w, y * 2 + 1 - core)

    def remote(src, dst, ssem, rsem, device):
        return pltpu.make_async_remote_copy(
            src_ref=src, dst_ref=dst, send_sem=ssem, recv_sem=rsem,
            device_id=device, device_id_type=MESH,
        )

    barrier = pltpu.get_barrier_semaphore()
    peers = [at_x(d) for d in (1, 2, 3)] + [at_z(d) for d in range(1, 8)]
    peers += [at_y(d) for d in (1, 2, 3)] + [other]
    for device in peers:
        pl.semaphore_signal(barrier, inc=1, device_id=device, device_id_type=MESH)

    def lanes1(xd, zd):
        return pl.ds(pl.multiple_of((xd * NZ + zd) * ROWS, 128), R1)

    def lanes2(xd, zd):
        return pl.ds(pl.multiple_of((xd * NZ + zd) * ROWS + R1, 128), R2)

    def own1(zd):
        return pltpu.make_async_copy(
            tail_ref.at[:, :, lanes1(x, zd)], a1.at[zd, x], a1_l.at[zd]
        )

    def own2(xd, far):
        zd = zpos(4 * far)
        return pltpu.make_async_copy(
            tail_ref.at[:, :, lanes2(xd, zd)],
            a2.at[far, 0, :, :, pl.ds(xd * R2, R2)], a2_l.at[far, xd],
        )

    for zd in range(NZ):
        own1(zd).start()
    for far in (0, 1):
        for xd in range(NX):
            own2(xd, far).start()

    def send1(d, zd):
        return remote(
            tail_ref.at[:, :, lanes1(xpos(d), zd)], a1.at[zd, x],
            a1_s.at[d, zd], a1_r.at[4 - d, zd], at_x(d),
        )

    def send2(i, xd, far):
        d = (1, -1, 2, -2)[i]
        zd = zpos(d + 4 * far)
        to = pl.ds(pl.multiple_of(xd * R2, R2), R2)
        if i < 2:
            src = tail_ref.at[:, :, lanes2(xd, zd)]
            dst = a2.at[far, 1 + i, :, :, to]
        else:
            src = tail_ref.at[far, :, lanes2(xd, zd)]
            dst = a2.at[far, 3, i - 2, :, to]
        return remote(src, dst, a2_s.at[i, far, xd], a2_r.at[i, far, xd], at_z(d))

    def each1(d, act):
        def body(zd, carry):
            act(send1(d, zd))
            return carry
        lax.fori_loop(0, NZ, body, 0)

    def each2(i, act):
        def body(xd, carry):
            for far in (0, 1):
                act(send2(i, xd, far))
            return carry
        lax.fori_loop(0, NX, body, 0)

    start = lambda copy: copy.start()
    sent = lambda copy: copy.wait_send()
    arrived = lambda copy: copy.wait_recv()

    crossT = cross_ref[...].T
    part[0] = dot(inv_ref[0], pl_ref[0])

    pl.semaphore_wait(barrier, len(peers))
    for d in (1, 2, 3):
        pl.semaphore_signal(known, inc=1, device_id=at_x(d), device_id_type=MESH)

    half = 32
    mine = pl.ds(pl.multiple_of(core * half, half), half)
    theirs = pl.ds(pl.multiple_of((1 - core) * half, half), half)

    def core_copy(p):
        return remote(part.at[p, theirs], corebuf.at[p], core_s.at[p], core_r.at[p], other)

    def y_copy(p, d):
        return remote(
            ybuf.at[p, y], ybuf.at[p, y], y_s.at[p, d], y_r.at[p, 4 - d], at_y(d)
        )

    def cg_copy(p):
        return remote(
            xg.at[x, p, mine], xg.at[x, p, mine], cg_s.at[p], cg_r.at[p], other
        )

    def gx_copy(p, d):
        return remote(
            xg.at[x, p], xg.at[x, p], gx_s.at[p, d], gx_r.at[p, 4 - d], at_x(d)
        )

    def gz_copy(p, i):
        d = (1, -1, 2, -2)[i]
        return remote(xg.at[x, p], xz.at[i, p], gz_s.at[p, i], gz_r.at[p, i], at_z(d))

    def sum_narrow(p, between):
        core_copy(p).start()
        between(0)
        core_copy(p).wait_recv()
        ybuf[p, y] = part[p, mine] + corebuf[p]
        for d in (2, 1, 3):
            y_copy(p, d).start()
        between(1)
        for d in (2, 1, 3):
            y_copy(p, d).wait_recv()
        xg[x, p, mine] = (ybuf[p, 0] + ybuf[p, 1]) + (ybuf[p, 2] + ybuf[p, 3])
        cg_copy(p).start()
        cg_copy(p).wait_recv()
        for d in (2, 1, 3):
            gx_copy(p, d).start()
        for i in (2, 3, 0, 1):
            gz_copy(p, i).start()
        sol_ref[p] = xg[x, p]

    def between_first(stage):
        if stage == 0:
            each1(2, start)
            each2(2, start)
            each2(3, start)
        else:
            each1(1, start)
            each1(3, start)
            each2(0, start)
            each2(1, start)

    sum_narrow(0, between_first)

    cpart[...] = dot(crossT, xg[x, 0])
    pl.semaphore_wait(known, 3)

    def rows_of(i):
        return pl.ds(pl.multiple_of(i * 8, 8), 8)

    def rs_copy(i):
        to = (w + i) % NW
        return remote(
            cpart.at[rows_of(to)], crecv.at[w], rs_s.at[i], rs_r.at[NW - i], (to, n)
        )

    def ag_copy(i):
        return remote(
            restall.at[rows_of(w)], restall.at[rows_of(w)], ag_s.at[i], ag_r.at[NW - i],
            ((w + i) % NW, n),
        )

    def each_peer(copy, act):
        def body(i, carry):
            act(copy(i))
            return carry
        lax.fori_loop(1, NW, body, 0)

    each_peer(rs_copy, start)
    crecv[w] = cpart[rows_of(w), :]
    each_peer(rs_copy, arrived)
    restall[rows_of(w), :] = pl_ref[1, rows_of(w), :] - jnp.sum(crecv[...], axis=0)
    each_peer(ag_copy, start)
    each_peer(ag_copy, arrived)

    part[1] = dot(inv_ref[1], restall[...])
    sum_narrow(1, lambda stage: None)

    for p in (0, 1):
        for d in (1, 2, 3):
            gx_copy(p, d).wait_recv()
        for i in range(4):
            gz_copy(p, i).wait_recv()

    def keep(which, value):
        hi, lo = split(value.T)
        xt[which, 0] = hi
        xt[which, 1] = lo

    keep(0, xg[...].reshape(512, 256))
    around = [xg[x].reshape(128, 256), xz[0].reshape(128, 256), xz[1].reshape(128, 256)]
    keep(1, jnp.concatenate(around + [xz[2, 0], xz[3, 0]], axis=0))
    keep(2, jnp.concatenate(around + [xz[2, 1], xz[3, 1]], axis=0))

    for i in range(4):
        each2(i, arrived)
    for far in (0, 1):
        for xd in range(NX):
            own2(xd, far).wait()

    def product2(far):
        value = dot3(xt[1 + far, 0], xt[1 + far, 1], a2[far].reshape(512, NX * R2))
        for xd in range(NX):
            qb[far, xd] = value[:, xd * R2:(xd + 1) * R2]

    H = (pl.ds(0, 128), pl.ds(128, 128))

    def x_first(far, way):
        return remote(
            qb.at[far, xpos(2), H[way]], xr0.at[far, way],
            b2_s.at[far, way, 0], b2_r.at[far, way, 0], at_x((1, -1)[way]),
        )

    def x_second(far, way):
        d = (1, -1)[way]
        return remote(
            qb.at[far, xpos(d)], xr1.at[far, way],
            b2_s.at[far, way, 1], b2_r.at[far, way, 1], at_x(d),
        )

    def z_copy(way, s, h):
        d = (-1, 1)[way]
        return remote(
            pb.at[zpos(d * (4 - s)), H[h]], recv1.at[way, s, H[h]],
            b1_s.at[way, s, h], b1_r.at[way, s, h], at_z(d),
        )

    def product1(d):
        zd = zpos(d)
        own1(zd).wait()
        for k in (1, 2, 3):
            send1(k, zd).wait_recv()
        pb[zd] = dot3(xt[0, 0], xt[0, 1], a1[zd].reshape(512, R1))

    def z_step(way, s):
        zd = zpos((-1, 1)[way] * (4 - s))
        halves = (way, 1 - way) if s == 1 else (way, 1 - way)
        for h in halves:
            if s > 1 or h == way:
                z_copy(way, s - 1, h).wait_recv()
                pb[zd, H[h], :] = pb[zd, H[h], :] + recv1[way, s - 1, H[h], :]
            z_copy(way, s, h).start()

    product1(4)
    z_copy(0, 0, 0).start()
    z_copy(1, 0, 1).start()
    product2(1)
    for way in (0, 1):
        x_first(1, way).start()
    product1(-3)
    product1(3)
    z_step(0, 1)
    z_step(1, 1)
    for way in (0, 1):
        x_first(1, way).wait_recv()
        spot = xpos((1, -1)[way])
        qb[1, spot, H[way], :] = qb[1, spot, H[way], :] + xr0[1, way]
        x_second(1, way).start()
    product2(0)
    for way in (0, 1):
        x_first(0, way).start()
    product1(-2)
    product1(2)
    z_step(0, 2)
    z_step(1, 2)
    for way in (0, 1):
        x_second(1, way).wait_recv()
    farsum[...] = qb[1, x] + (xr1[1, 0] + xr1[1, 1])
    far_copy = remote(farsum, farrecv, b3_s.at[0], b3_r.at[0], at_z(4))
    far_copy.start()
    for way in (0, 1):
        x_first(0, way).wait_recv()
        spot = xpos((1, -1)[way])
        qb[0, spot, H[way], :] = qb[0, spot, H[way], :] + xr0[0, way]
        x_second(0, way).start()
    product1(-1)
    product1(1)
    z_step(0, 3)
    z_step(1, 3)
    product1(0)
    for way in (0, 1):
        x_second(0, way).wait_recv()
    far_copy.wait_recv()
    total2 = qb[0, x] + (xr1[0, 0] + xr1[0, 1]) + farrecv[...]
    out_ref[R1:, :] = loads_ref[R1:, :] - total2.T
    for way in (0, 1):
        for h in (0, 1):
            z_copy(way, 3, h).wait_recv()
    total1 = pb[z] + (recv1[0, 3] + recv1[1, 3])
    out_ref[:R1, :] = loads_ref[:R1, :] - total1.T

    for p in (0, 1):
        core_copy(p).wait_send()
        cg_copy(p).wait_send()
        for d in (1, 2, 3):
            y_copy(p, d).wait_send()
            gx_copy(p, d).wait_send()
        for i in range(4):
            gz_copy(p, i).wait_send()
    each_peer(rs_copy, sent)
    each_peer(ag_copy, sent)
    for d in (1, 2, 3):
        each1(d, sent)
    for i in range(4):
        each2(i, sent)
    for far in (0, 1):
        for way in (0, 1):
            x_first(far, way).wait_send()
            x_second(far, way).wait_send()
    z_copy(0, 0, 0).wait_send()
    z_copy(1, 0, 1).wait_send()
    for way in (0, 1):
        for s in (1, 2, 3):
            for h in (0, 1):
                z_copy(way, s, h).wait_send()
    far_copy.wait_send()


def on_device(panel_loads, tail_loads, inverses, cross_factor, tail_factor):
    vmem = pl.BlockSpec(memory_space=pltpu.VMEM)
    dma = pltpu.SemaphoreType.DMA
    scratch = [
        pltpu.VMEM((2, 64, 256), F32),
        pltpu.VMEM((2, 32, 256), F32),
        pltpu.VMEM((2, NY, 32, 256), F32),
        pltpu.VMEM((NX, 2, 64, 256), F32),
        pltpu.VMEM((4, 2, 64, 256), F32),
        pltpu.VMEM((256, 256), F32),
        pltpu.VMEM((NW, 8, 256), F32),
        pltpu.VMEM((256, 256), F32),
        pltpu.VMEM((NZ, NX, 2, 64, R1), F32),
        pltpu.VMEM((2, 4, 2, 64, NX * R2), F32),
        pltpu.VMEM((NZ, 256, R1), F32),
        pltpu.VMEM((2, NX, 256, R2), F32),
        pltpu.VMEM((2, 4, 256, R1), F32),
        pltpu.VMEM((2, 2, 128, R2), F32),
        pltpu.VMEM((2, 2, 256, R2), F32),
        pltpu.VMEM((256, R2), F32),
        pltpu.VMEM((256, R2), F32),
        pltpu.VMEM((3, 2, 256, 512), BF16),
        dma((2,)), dma((2,)), dma((2, 4)), dma((2, 4)), dma((2,)), dma((2,)),
        pltpu.SemaphoreType.REGULAR,
        dma((NW,)), dma((NW,)), dma((NW,)), dma((NW,)),
        dma((2, 4)), dma((2, 4)), dma((2, 4)), dma((2, 4)),
        dma((4, NZ)), dma((4, NZ)), dma((NZ,)),
        dma((4, 2, NX)), dma((4, 2, NX)), dma((2, NX)),
        dma((2, 4, 2)), dma((2, 4, 2)), dma((2, 2, 2)), dma((2, 2, 2)), dma((1,)), dma((1,)),
    ]
    return pl.pallas_call(
        kernel,
        out_shape=(
            jax.ShapeDtypeStruct((2, 64, 256), F32),
            jax.ShapeDtypeStruct((ROWS, 256), F32),
        ),
        in_specs=[vmem, vmem, vmem, vmem, pl.BlockSpec(memory_space=pl.ANY)],
        out_specs=(vmem, vmem),
        scratch_shapes=scratch,
        compiler_params=pltpu.CompilerParams(
            collective_id=0, has_side_effects=True, vmem_limit_bytes=48 * 1024 * 1024
        ),
    )(panel_loads, inverses, cross_factor, tail_loads, tail_factor)


def solution(mesh):
    in_specs = (
        P(None, "narrow", None),
        P(("narrow", "wide"), None),
        P(None, "wide", "narrow"),
        P("wide", "narrow"),
        P(None, "wide", "narrow"),
    )
    out_specs = (P(None, "wide", None), P(("narrow", "wide"), None))
    return jax.shard_map(
        on_device, mesh=mesh, in_specs=in_specs, out_specs=out_specs, check_vma=False
    )
```

```python
import functools

import jax
import jax.numpy as jnp
from jax import lax
from jax.experimental import pallas as pl
from jax.experimental.pallas import tpu as pltpu
from jax.sharding import PartitionSpec as P

MESH = pl.DeviceIdType.MESH
NX, NZ, NY = 4, 8, 4
NW = NX * NZ
ROWS = 384
R1 = 256
R2 = 128
HIGH = lax.Precision.HIGHEST
F32 = jnp.float32
BF16 = jnp.bfloat16
SCHEDULE = {
    0: ((1, 0, 1),),
    1: ((1, 1, 2), (2, 0, 1)),
    2: (),
    3: ((1, 2, 3), (2, 1, 2)),
    4: ((1, 3, 4), (2, 2, 3)),
    6: (),
    7: ((1, 4, 5), (2, 3, 4)),
    8: ((1, 5, 6),),
    9: ((1, 6, 7),),
    10: ((1, 7, 8),),
}


def dot(a, b):
    return jnp.dot(a, b, precision=HIGH, preferred_element_type=F32)


def split(a):
    hi = a.astype(BF16)
    return hi, (a - hi.astype(F32)).astype(BF16)


def dot3(xh, xl, a):
    ah, al = split(a)
    out = jnp.dot(xh, ah, preferred_element_type=F32)
    out += jnp.dot(xl, ah, preferred_element_type=F32)
    return out + jnp.dot(xh, al, preferred_element_type=F32)


def kernel(
    pl_hbm, inv_hbm, cross_hbm, loads_hbm, tail_ref,
    sol_ref, out_ref,
    pl_ref, inv_ref, cross_ref, loads_ref,
    part, corebuf, ybuf, xg, xz, cpart, crecv, restall,
    a1, a2, pb, qb, recv1, xr0, xr1, farsum, farrecv, xt,
    core_s, core_r, y_s, y_r, cg_s, cg_r, known,
    rs_s, rs_r, ag_s, ag_r, gx_s, gx_r, gz_s, gz_r, fx_s, fx_r, fz_s, fz_r,
    a1_s, a1_r, a1_l, a2_s, a2_r, a2_l,
    b1_s, b1_r, b2_s, b2_r, b3_s, b3_r, load,
):
    w = lax.axis_index("wide")
    n = lax.axis_index("narrow")
    x, z = w // NZ, w % NZ
    y, core = n // 2, n % 2

    def xpos(d):
        return (x + d + NX) % NX

    def zpos(d):
        return (z + d + NZ) % NZ

    def at_x(d):
        return (xpos(d) * NZ + z, n)

    def at_z(d):
        return (x * NZ + zpos(d), n)

    def at_y(d):
        return (w, ((y + d) % NY) * 2 + core)

    other = (w, y * 2 + 1 - core)

    def remote(src, dst, ssem, rsem, device):
        return pltpu.make_async_remote_copy(
            src_ref=src, dst_ref=dst, send_sem=ssem, recv_sem=rsem,
            device_id=device, device_id_type=MESH,
        )

    barrier = pltpu.get_barrier_semaphore()
    peers = [at_x(d) for d in (1, 2, 3)] + [at_z(d) for d in (1, -1, 2, -2)]
    peers += [at_y(d) for d in (1, 2, 3)] + [other]
    for device in peers:
        pl.semaphore_signal(barrier, inc=1, device_id=device, device_id_type=MESH)

    loads = [
        pltpu.make_async_copy(src, dst, load.at[i])
        for i, (src, dst) in enumerate((
            (pl_hbm, pl_ref), (inv_hbm, inv_ref), (cross_hbm, cross_ref), (loads_hbm, loads_ref),
        ))
    ]
    for copy in loads:
        copy.start()

    def lanes1(xd, zd):
        return pl.ds(pl.multiple_of((xd * NZ + zd) * ROWS, 128), R1)

    def lanes2(xd, zd):
        return pl.ds(pl.multiple_of((xd * NZ + zd) * ROWS + R1, 128), R2)

    def own1(zd):
        return pltpu.make_async_copy(
            tail_ref.at[:, :, lanes1(x, zd)], a1.at[zd, :, x], a1_l.at[zd]
        )

    def own2(xd, far):
        zd = zpos(4 * far)
        return pltpu.make_async_copy(
            tail_ref.at[:, :, lanes2(xd, zd)],
            a2.at[far, 0, :, :, pl.ds(pl.multiple_of(xd * R2, R2), R2)], a2_l.at[far, xd],
        )

    def send1(d, zd):
        return remote(
            tail_ref.at[:, :, lanes1(xpos(d), zd)], a1.at[zd, :, x],
            a1_s.at[d, zd], a1_r.at[4 - d, zd], at_x(d),
        )

    def send2(i, xd, far):
        d = (1, -1, 2, -2)[i]
        zd = zpos(d + 4 * far)
        to = pl.ds(pl.multiple_of(xd * R2, R2), R2)
        if i < 2:
            src = tail_ref.at[:, :, lanes2(xd, zd)]
            dst = a2.at[far, 1 + i, :, :, to]
        else:
            src = tail_ref.at[far, :, lanes2(xd, zd)]
            dst = a2.at[far, 3, i - 2, :, to]
        return remote(src, dst, a2_s.at[i, far, xd], a2_r.at[i, far, xd], at_z(d))

    def feed1(first, last):
        def body(i, carry):
            zd = zpos((4 - (i + 1) // 2) * (1 - 2 * (i % 2)))
            for d in (2, 1, 3):
                send1(d, zd).start()
            own1(zd).start()
            return carry
        lax.fori_loop(first, last, body, 0)

    def feed2(first, last):
        def body(xd, carry):
            for far in (1, 0):
                for i in (2, 3, 0, 1):
                    send2(i, xd, far).start()
                own2(xd, far).start()
            return carry
        lax.fori_loop(first, last, body, 0)

    def feed(stage):
        for kind, first, last in SCHEDULE[stage]:
            (feed1 if kind == 1 else feed2)(first, last)

    def each1(d, act):
        def body(zd, carry):
            act(send1(d, zd))
            return carry
        lax.fori_loop(0, NZ, body, 0)

    def each2(i, act):
        def body(xd, carry):
            for far in (0, 1):
                act(send2(i, xd, far))
            return carry
        lax.fori_loop(0, NX, body, 0)

    start = lambda copy: copy.start()
    sent = lambda copy: copy.wait_send()
    arrived = lambda copy: copy.wait_recv()

    for copy in loads:
        copy.wait()
    crossT = cross_ref[...].T
    part[0] = dot(inv_ref[0], pl_ref[0])

    pl.semaphore_wait(barrier, len(peers))
    for d in (1, 2, 3):
        pl.semaphore_signal(known.at[0], inc=1, device_id=at_x(d), device_id_type=MESH)

    half = 32
    mine = pl.ds(pl.multiple_of(core * half, half), half)
    theirs = pl.ds(pl.multiple_of((1 - core) * half, half), half)

    def core_copy(p):
        return remote(part.at[p, theirs], corebuf.at[p], core_s.at[p], core_r.at[p], other)

    def y_copy(p, d):
        return remote(
            ybuf.at[p, y], ybuf.at[p, y], y_s.at[p, d], y_r.at[p, 4 - d], at_y(d)
        )

    def cg_copy(p):
        return remote(
            xg.at[x, p, mine], xg.at[x, p, mine], cg_s.at[p], cg_r.at[p], other
        )

    def gx_copy(p, d):
        return remote(
            xg.at[x, p, mine], xg.at[x, p, mine], gx_s.at[p, d], gx_r.at[p, 4 - d], at_x(d)
        )

    def gz_copy(p, i):
        d = (1, -1, 2, -2)[i]
        return remote(
            xg.at[x, p, mine], xz.at[i, p, mine], gz_s.at[p, i], gz_r.at[p, i], at_z(d)
        )

    def fx_copy(p, d):
        return remote(
            xg.at[xpos(d), p, mine], xg.at[xpos(d), p, mine],
            fx_s.at[p, d], fx_r.at[p, d], other,
        )

    def fz_copy(p, i):
        return remote(
            xz.at[i, p, mine], xz.at[i, p, mine], fz_s.at[p, i], fz_r.at[p, i], other
        )

    def pass_on(p):
        for d in (1, 3, 2):
            gx_copy(p, 4 - d).wait_recv()
            fx_copy(p, d).start()
        for i in range(4):
            gz_copy(p, i).wait_recv()
            fz_copy(p, i).start()

    def sum_narrow(p):
        core_copy(p).start()
        feed(6 * p)
        core_copy(p).wait_recv()
        ybuf[p, y] = part[p, mine] + corebuf[p]
        for d in (2, 1, 3):
            y_copy(p, d).start()
        feed(6 * p + 1)
        for d in (2, 1, 3):
            y_copy(p, d).wait_recv()
        xg[x, p, mine] = (ybuf[p, 0] + ybuf[p, 1]) + (ybuf[p, 2] + ybuf[p, 3])
        cg_copy(p).start()
        for d in (2, 1, 3):
            gx_copy(p, d).start()
        for i in (2, 3, 0, 1):
            gz_copy(p, i).start()
        feed(6 * p + 2)
        cg_copy(p).wait_recv()

    sum_narrow(0)
    pl.semaphore_wait(known.at[0], 3)
    for d in (2, -2):
        pl.semaphore_signal(known.at[1], inc=1, device_id=at_z(d), device_id_type=MESH)

    def keep(which, spot, value):
        hi, lo = split(value.T)
        xt[which, 0, :, spot] = hi
        xt[which, 1, :, spot] = lo

    def keep_x(p):
        for d in (1, 2, 3):
            fx_copy(p, d).wait_recv()
        keep(0, pl.ds(p * 256, 256), xg[:, p].reshape(256, 256))

    cpart[...] = dot(crossT, xg[x, 0])
    pl.semaphore_wait(known.at[1], 2)

    def rows_of(i):
        return pl.ds(pl.multiple_of(i * 8, 8), 8)

    def peer(j):
        dz = (4 - (j // 4 + 1) // 2) * (1 - 2 * (j // 4 % 2))
        q = j % 4
        dx = 2 + (q + 1) // 2 * (1 - 2 * (q % 2))
        return xpos(dx) * NZ + zpos(dz)

    def rs_copy(j):
        to = peer(j)
        return remote(cpart.at[rows_of(to)], crecv.at[w], rs_s.at[j], rs_r.at[j], (to, n))

    def ag_copy(j):
        return remote(
            restall.at[rows_of(w)], restall.at[rows_of(w)], ag_s.at[j], ag_r.at[j], (peer(j), n)
        )

    def each_peer(copy, act):
        def body(i, carry):
            act(copy(i))
            return carry
        lax.fori_loop(0, NW - 1, body, 0)

    each_peer(rs_copy, start)
    feed(3)
    crecv[w] = cpart[rows_of(w), :]
    each_peer(rs_copy, arrived)
    restall[rows_of(w), :] = pl_ref[1, rows_of(w), :] - jnp.sum(crecv[...], axis=0)
    each_peer(ag_copy, start)
    feed(4)
    pass_on(0)
    sol_ref[0] = xg[x, 0]
    keep_x(0)
    each_peer(ag_copy, arrived)

    part[1] = dot(inv_ref[1], restall[...])
    sum_narrow(1)

    def keep_z():
        for p in (0, 1):
            for i in range(4):
                fz_copy(p, i).wait_recv()
        around = [xg[x].reshape(128, 256), xz[0].reshape(128, 256), xz[1].reshape(128, 256)]
        keep(1, pl.ds(0, 512), jnp.concatenate(around + [xz[2, 0], xz[3, 0]], axis=0))
        keep(2, pl.ds(0, 512), jnp.concatenate(around + [xz[2, 1], xz[3, 1]], axis=0))
        for i in range(4):
            each2(i, arrived)
        for far in (0, 1):
            for xd in range(NX):
                own2(xd, far).wait()

    def product2(far):
        value = dot3(xt[1 + far, 0], xt[1 + far, 1], a2[far].reshape(512, NX * R2))
        for xd in range(NX):
            qb[far, xd] = value[:, xd * R2:(xd + 1) * R2]

    H = (pl.ds(0, 128), pl.ds(128, 128))

    def x_first(far, way):
        return remote(
            qb.at[far, xpos(2), H[way]], xr0.at[far, way],
            b2_s.at[far, way, 0], b2_r.at[far, way, 0], at_x((1, -1)[way]),
        )

    def x_second(far, way):
        d = (1, -1)[way]
        return remote(
            qb.at[far, xpos(d)], xr1.at[far, way],
            b2_s.at[far, way, 1], b2_r.at[far, way, 1], at_x(d),
        )

    def z_copy(way, s, h):
        d = (-1, 1)[way]
        return remote(
            pb.at[zpos(d * (4 - s)), H[h]], recv1.at[way, s, H[h]],
            b1_s.at[way, s, h], b1_r.at[way, s, h], at_z(d),
        )

    def product1(d):
        zd = zpos(d)
        own1(zd).wait()
        for k in (1, 2, 3):
            send1(k, zd).wait_recv()
        pb[zd] = dot3(xt[0, 0], xt[0, 1], a1[zd].reshape(512, R1))

    def z_step(way, s):
        zd = zpos((-1, 1)[way] * (4 - s))
        halves = (1 - way, way) if s == 1 else (way, 1 - way)
        for h in halves:
            if s > 1 or h == way:
                z_copy(way, s - 1, h).wait_recv()
                pb[zd, H[h], :] = pb[zd, H[h], :] + recv1[way, s - 1, H[h], :]
            z_copy(way, s, h).start()

    pass_on(1)
    sol_ref[1] = xg[x, 1]
    keep_x(1)
    product1(4)
    z_copy(0, 0, 0).start()
    z_copy(1, 0, 1).start()
    keep_z()
    product2(1)
    for way in (0, 1):
        x_first(1, way).start()
    feed(9)
    product1(-3)
    product1(3)
    z_step(0, 1)
    z_step(1, 1)
    for way in (0, 1):
        x_first(1, way).wait_recv()
        spot = xpos((1, -1)[way])
        qb[1, spot, H[way], :] = qb[1, spot, H[way], :] + xr0[1, way]
        x_second(1, way).start()
    feed(10)
    product2(0)
    for way in (0, 1):
        x_first(0, way).start()
    product1(-2)
    product1(2)
    z_step(0, 2)
    z_step(1, 2)
    for way in (0, 1):
        x_second(1, way).wait_recv()
    farsum[...] = qb[1, x] + (xr1[1, 0] + xr1[1, 1])
    far_copy = remote(farsum, farrecv, b3_s.at[0], b3_r.at[0], at_z(4))
    far_copy.start()
    for way in (0, 1):
        x_first(0, way).wait_recv()
        spot = xpos((1, -1)[way])
        qb[0, spot, H[way], :] = qb[0, spot, H[way], :] + xr0[0, way]
        x_second(0, way).start()
    product1(-1)
    product1(1)
    z_step(0, 3)
    z_step(1, 3)
    product1(0)
    for way in (0, 1):
        x_second(0, way).wait_recv()
    far_copy.wait_recv()
    total2 = qb[0, x] + (xr1[0, 0] + xr1[0, 1]) + farrecv[...]
    out_ref[R1:, :] = loads_ref[R1:, :] - total2.T
    for way in (0, 1):
        for h in (0, 1):
            z_copy(way, 3, h).wait_recv()
    total1 = pb[z] + (recv1[0, 3] + recv1[1, 3])
    out_ref[:R1, :] = loads_ref[:R1, :] - total1.T

    for p in (0, 1):
        core_copy(p).wait_send()
        cg_copy(p).wait_send()
        for d in (1, 2, 3):
            y_copy(p, d).wait_send()
            gx_copy(p, d).wait_send()
            fx_copy(p, d).wait_send()
        for i in range(4):
            gz_copy(p, i).wait_send()
            fz_copy(p, i).wait_send()
    each_peer(rs_copy, sent)
    each_peer(ag_copy, sent)
    for d in (1, 2, 3):
        each1(d, sent)
    for i in range(4):
        each2(i, sent)
    for far in (0, 1):
        for way in (0, 1):
            x_first(far, way).wait_send()
            x_second(far, way).wait_send()
    z_copy(0, 0, 0).wait_send()
    z_copy(1, 0, 1).wait_send()
    for way in (0, 1):
        for s in (1, 2, 3):
            for h in (0, 1):
                z_copy(way, s, h).wait_send()
    far_copy.wait_send()


def on_device(panel_loads, tail_loads, inverses, cross_factor, tail_factor):
    vmem = pl.BlockSpec(memory_space=pltpu.VMEM)
    dma = pltpu.SemaphoreType.DMA
    scratch = [
        pltpu.VMEM((2, 256, 256), F32),
        pltpu.VMEM((2, 64, 256), F32),
        pltpu.VMEM((64, 256), F32),
        pltpu.VMEM((ROWS, 256), F32),
        pltpu.VMEM((2, 64, 256), F32),
        pltpu.VMEM((2, 32, 256), F32),
        pltpu.VMEM((2, NY, 32, 256), F32),
        pltpu.VMEM((NX, 2, 64, 256), F32),
        pltpu.VMEM((4, 2, 64, 256), F32),
        pltpu.VMEM((256, 256), F32),
        pltpu.VMEM((NW, 8, 256), F32),
        pltpu.VMEM((256, 256), F32),
        pltpu.VMEM((NZ, 2, NX, 64, R1), F32),
        pltpu.VMEM((2, 4, 2, 64, NX * R2), F32),
        pltpu.VMEM((NZ, 256, R1), F32),
        pltpu.VMEM((2, NX, 256, R2), F32),
        pltpu.VMEM((2, 4, 256, R1), F32),
        pltpu.VMEM((2, 2, 128, R2), F32),
        pltpu.VMEM((2, 2, 256, R2), F32),
        pltpu.VMEM((256, R2), F32),
        pltpu.VMEM((256, R2), F32),
        pltpu.VMEM((3, 2, 256, 512), BF16),
        dma((2,)), dma((2,)), dma((2, 4)), dma((2, 4)), dma((2,)), dma((2,)),
        pltpu.SemaphoreType.REGULAR((2,)),
        dma((NW,)), dma((NW,)), dma((NW,)), dma((NW,)),
        dma((2, 4)), dma((2, 4)), dma((2, 4)), dma((2, 4)),
        dma((2, 4)), dma((2, 4)), dma((2, 4)), dma((2, 4)),
        dma((4, NZ)), dma((4, NZ)), dma((NZ,)),
        dma((4, 2, NX)), dma((4, 2, NX)), dma((2, NX)),
        dma((2, 4, 2)), dma((2, 4, 2)), dma((2, 2, 2)), dma((2, 2, 2)), dma((1,)), dma((1,)), dma((4,)),
    ]
    return pl.pallas_call(
        kernel,
        out_shape=(
            jax.ShapeDtypeStruct((2, 64, 256), F32),
            jax.ShapeDtypeStruct((ROWS, 256), F32),
        ),
        in_specs=[pl.BlockSpec(memory_space=pl.ANY)] * 5,
        out_specs=(vmem, vmem),
        scratch_shapes=scratch,
        compiler_params=pltpu.CompilerParams(
            collective_id=0, has_side_effects=True, vmem_limit_bytes=56 * 1024 * 1024
        ),
    )(panel_loads, inverses, cross_factor, tail_loads, tail_factor)


def solution(mesh):
    in_specs = (
        P(None, "narrow", None),
        P(("narrow", "wide"), None),
        P(None, "wide", "narrow"),
        P("wide", "narrow"),
        P(None, "wide", "narrow"),
    )
    out_specs = (P(None, "wide", None), P(("narrow", "wide"), None))
    return jax.shard_map(
        on_device, mesh=mesh, in_specs=in_specs, out_specs=out_specs, check_vma=False
    )
```

```python
import functools

import jax
import jax.numpy as jnp
from jax import lax
from jax.experimental import pallas as pl
from jax.experimental.pallas import tpu as pltpu
from jax.sharding import PartitionSpec as P

MESH = pl.DeviceIdType.MESH
NX, NZ, NY = 4, 8, 4
NW = NX * NZ
ROWS = 384
R1 = 256
R2 = 128
HIGH = lax.Precision.HIGHEST
F32 = jnp.float32
BF16 = jnp.bfloat16
SCHEDULE = {
    0: ((1, 0, 1), (2, 0, 1)),
    1: ((1, 1, 2),),
    2: (),
    3: ((1, 2, 3), (2, 1, 2)),
    4: ((1, 3, 4), (2, 2, 3)),
    6: ((2, 3, 4),),
    7: ((1, 4, 5),),
    8: ((1, 5, 6),),
    9: ((1, 6, 7),),
    10: ((1, 7, 8),),
}


def dot(a, b):
    return jnp.dot(a, b, precision=HIGH, preferred_element_type=F32)


def split(a):
    hi = a.astype(BF16)
    return hi, (a - hi.astype(F32)).astype(BF16)


def dot3(xh, xl, a):
    ah, al = split(a)
    out = jnp.dot(xh, ah, preferred_element_type=F32)
    out += jnp.dot(xl, ah, preferred_element_type=F32)
    return out + jnp.dot(xh, al, preferred_element_type=F32)


def kernel(
    pl_hbm, inv_hbm, cross_hbm, loads_hbm, tail_ref,
    sol_ref, out_ref,
    pl_ref, inv_ref, cross_ref, loads_ref,
    part, corebuf, ybuf, xg, xz, cpart, crecv, restall,
    a1, a2, pb, qb, recv1, xr0, xr1, farsum, farrecv, xt,
    core_s, core_r, y_s, y_r, cg_s, cg_r, known,
    rs_s, rs_r, ag_s, ag_r, gx_s, gx_r, gz_s, gz_r, fx_s, fx_r, fz_s, fz_r,
    a1_s, a1_r, a1_l, a2_s, a2_r, a2_l,
    b1_s, b1_r, b2_s, b2_r, b3_s, b3_r, load,
):
    w = lax.axis_index("wide")
    n = lax.axis_index("narrow")
    x, z = w // NZ, w % NZ
    y, core = n // 2, n % 2

    def xpos(d):
        return (x + d + NX) % NX

    def zpos(d):
        return (z + d + NZ) % NZ

    def at_x(d):
        return (xpos(d) * NZ + z, n)

    def at_z(d):
        return (x * NZ + zpos(d), n)

    def at_y(d):
        return (w, ((y + d) % NY) * 2 + core)

    other = (w, y * 2 + 1 - core)

    def remote(src, dst, ssem, rsem, device):
        return pltpu.make_async_remote_copy(
            src_ref=src, dst_ref=dst, send_sem=ssem, recv_sem=rsem,
            device_id=device, device_id_type=MESH,
        )

    barrier = pltpu.get_barrier_semaphore()
    peers = [at_x(d) for d in (1, 2, 3)] + [at_z(d) for d in (1, -1, 2, -2)]
    peers += [at_y(d) for d in (1, 2, 3)] + [other]
    for device in peers:
        pl.semaphore_signal(barrier, inc=1, device_id=device, device_id_type=MESH)

    loads = [
        pltpu.make_async_copy(src, dst, load.at[i])
        for i, (src, dst) in enumerate((
            (pl_hbm, pl_ref), (inv_hbm, inv_ref), (cross_hbm, cross_ref), (loads_hbm, loads_ref),
        ))
    ]
    for copy in loads:
        copy.start()

    def lanes1(xd, zd):
        return pl.ds(pl.multiple_of((xd * NZ + zd) * ROWS, 128), R1)

    def lanes2(xd, zd):
        return pl.ds(pl.multiple_of((xd * NZ + zd) * ROWS + R1, 128), R2)

    def own1(zd):
        return pltpu.make_async_copy(
            tail_ref.at[:, :, lanes1(x, zd)], a1.at[zd, :, x], a1_l.at[zd]
        )

    def own2(xd, far):
        zd = zpos(4 * far)
        return pltpu.make_async_copy(
            tail_ref.at[:, :, lanes2(xd, zd)],
            a2.at[far, 0, :, :, pl.ds(pl.multiple_of(xd * R2, R2), R2)], a2_l.at[far, xd],
        )

    def send1(d, zd):
        return remote(
            tail_ref.at[:, :, lanes1(xpos(d), zd)], a1.at[zd, :, x],
            a1_s.at[0], a1_r.at[zd], at_x(d),
        )

    def send2(i, xd, far):
        d = (1, -1, 2, -2)[i]
        zd = zpos(d + 4 * far)
        to = pl.ds(pl.multiple_of(xd * R2, R2), R2)
        if i < 2:
            src = tail_ref.at[:, :, lanes2(xd, zd)]
            dst = a2.at[far, 1 + i, :, :, to]
        else:
            src = tail_ref.at[far, :, lanes2(xd, zd)]
            dst = a2.at[far, 3, i - 2, :, to]
        return remote(src, dst, a2_s.at[0], a2_r.at[0], at_z(d))

    def feed1(first, last):
        def body(i, carry):
            zd = zpos((4 - (i + 1) // 2) * (1 - 2 * (i % 2)))
            for d in (2, 1, 3):
                send1(d, zd).start()
            own1(zd).start()
            return carry
        lax.fori_loop(first, last, body, 0)

    def feed2(first, last):
        def body(xd, carry):
            for far in (1, 0):
                for i in (2, 3, 0, 1):
                    send2(i, xd, far).start()
                own2(xd, far).start()
            return carry
        lax.fori_loop(first, last, body, 0)

    def feed(stage):
        for kind, first, last in SCHEDULE[stage]:
            (feed1 if kind == 1 else feed2)(first, last)

    def whole(like, sem):
        pltpu.make_async_copy(like, like, sem).wait()

    for copy in loads:
        copy.wait()
    crossT = cross_ref[...].T
    part[0] = dot(inv_ref[0], pl_ref[0])

    pl.semaphore_wait(barrier, len(peers))
    for d in (1, 2, 3):
        pl.semaphore_signal(known.at[0], inc=1, device_id=at_x(d), device_id_type=MESH)

    half = 32
    mine = pl.ds(pl.multiple_of(core * half, half), half)
    theirs = pl.ds(pl.multiple_of((1 - core) * half, half), half)

    def core_copy(p):
        return remote(part.at[p, theirs], corebuf.at[p], core_s.at[p], core_r.at[p], other)

    def y_copy(p, d):
        return remote(
            ybuf.at[p, y], ybuf.at[p, y], y_s.at[p, d], y_r.at[p, 4 - d], at_y(d)
        )

    def cg_copy(p):
        return remote(
            xg.at[x, p, mine], xg.at[x, p, mine], cg_s.at[p], cg_r.at[p], other
        )

    def gx_copy(p, d):
        return remote(
            xg.at[x, p, mine], xg.at[x, p, mine], gx_s.at[p, d], gx_r.at[p, 4 - d], at_x(d)
        )

    def gz_copy(p, i):
        d = (1, -1, 2, -2)[i]
        return remote(
            xg.at[x, p, mine], xz.at[i, p, mine], gz_s.at[p, i], gz_r.at[p, i], at_z(d)
        )

    def fx_copy(p, d):
        return remote(
            xg.at[xpos(d), p, mine], xg.at[xpos(d), p, mine],
            fx_s.at[p, d], fx_r.at[p, d], other,
        )

    def fz_copy(p, i):
        return remote(
            xz.at[i, p, mine], xz.at[i, p, mine], fz_s.at[p, i], fz_r.at[p, i], other
        )

    def pass_on(p):
        for d in (1, 3, 2):
            gx_copy(p, 4 - d).wait_recv()
            fx_copy(p, d).start()
        for i in range(4):
            gz_copy(p, i).wait_recv()
            fz_copy(p, i).start()

    def sum_narrow(p):
        core_copy(p).start()
        feed(6 * p)
        core_copy(p).wait_recv()
        ybuf[p, y] = part[p, mine] + corebuf[p]
        for d in (2, 1, 3):
            y_copy(p, d).start()
        if p == 0:
            pl.semaphore_wait(known.at[0], 3)
            for d in (2, -2):
                pl.semaphore_signal(
                    known.at[1], inc=1, device_id=at_z(d), device_id_type=MESH
                )
        feed(6 * p + 1)
        for d in (2, 1, 3):
            y_copy(p, d).wait_recv()
        xg[x, p, mine] = (ybuf[p, 0] + ybuf[p, 1]) + (ybuf[p, 2] + ybuf[p, 3])
        cg_copy(p).start()
        for d in (2, 1, 3):
            gx_copy(p, d).start()
        for i in (2, 3, 0, 1):
            gz_copy(p, i).start()
        feed(6 * p + 2)
        cg_copy(p).wait_recv()

    sum_narrow(0)

    def keep(which, spot, value):
        hi, lo = split(value.T)
        xt[which, 0, :, spot] = hi
        xt[which, 1, :, spot] = lo

    def keep_x(p):
        for d in (1, 2, 3):
            fx_copy(p, d).wait_recv()
        keep(0, pl.ds(p * 256, 256), xg[:, p].reshape(256, 256))

    cpart[...] = dot(crossT, xg[x, 0])
    pl.semaphore_wait(known.at[1], 2)

    def rows_of(i):
        return pl.ds(pl.multiple_of(i * 8, 8), 8)

    def peer(j):
        dz = (4 - (j // 4 + 1) // 2) * (1 - 2 * (j // 4 % 2))
        q = j % 4
        dx = 2 + (q + 1) // 2 * (1 - 2 * (q % 2))
        return xpos(dx) * NZ + zpos(dz)

    def rs_copy(j):
        to = peer(j)
        return remote(cpart.at[rows_of(to)], crecv.at[w], rs_s.at[0], rs_r.at[0], (to, n))

    def ag_copy(j):
        return remote(
            restall.at[rows_of(w)], restall.at[rows_of(w)], ag_s.at[0], ag_r.at[0], (peer(j), n)
        )

    def to_peers(copy):
        def body(j, carry):
            copy(j).start()
            return carry
        lax.fori_loop(0, NW - 1, body, 0)

    to_peers(rs_copy)
    feed(3)
    crecv[w] = cpart[rows_of(w), :]
    whole(crecv.at[pl.ds(0, NW - 1)], rs_r.at[0])
    restall[rows_of(w), :] = pl_ref[1, rows_of(w), :] - jnp.sum(crecv[...], axis=0)
    to_peers(ag_copy)
    feed(4)
    pass_on(0)
    sol_ref[0] = xg[x, 0]
    keep_x(0)
    whole(restall.at[pl.ds(0, 8 * (NW - 1))], ag_r.at[0])

    part[1] = dot(inv_ref[1], restall[...])
    sum_narrow(1)

    def keep_z():
        for p in (0, 1):
            for i in range(4):
                fz_copy(p, i).wait_recv()
        around = [xg[x].reshape(128, 256), xz[0].reshape(128, 256), xz[1].reshape(128, 256)]
        keep(1, pl.ds(0, 512), jnp.concatenate(around + [xz[2, 0], xz[3, 0]], axis=0))
        keep(2, pl.ds(0, 512), jnp.concatenate(around + [xz[2, 1], xz[3, 1]], axis=0))
        whole(a2.at[:, pl.ds(0, 3)], a2_r.at[0])
        for far in (0, 1):
            for xd in range(NX):
                own2(xd, far).wait()

    def product2(far):
        value = dot3(xt[1 + far, 0], xt[1 + far, 1], a2[far].reshape(512, NX * R2))
        for xd in range(NX):
            qb[far, xd] = value[:, xd * R2:(xd + 1) * R2]

    H = (pl.ds(0, 128), pl.ds(128, 128))

    def x_first(far, way):
        return remote(
            qb.at[far, xpos(2), H[way]], xr0.at[far, way],
            b2_s.at[far, way, 0], b2_r.at[far, way, 0], at_x((1, -1)[way]),
        )

    def x_second(far, way):
        d = (1, -1)[way]
        return remote(
            qb.at[far, xpos(d)], xr1.at[far, way],
            b2_s.at[far, way, 1], b2_r.at[far, way, 1], at_x(d),
        )

    def z_copy(way, s, h):
        d = (-1, 1)[way]
        return remote(
            pb.at[zpos(d * (4 - s)), H[h]], recv1.at[way, s, H[h]],
            b1_s.at[way, s, h], b1_r.at[way, s, h], at_z(d),
        )

    def product1(d):
        zd = zpos(d)
        own1(zd).wait()
        whole(a1.at[zd, :, pl.ds(0, NX - 1)], a1_r.at[zd])
        pb[zd] = dot3(xt[0, 0], xt[0, 1], a1[zd].reshape(512, R1))

    def z_step(way, s):
        zd = zpos((-1, 1)[way] * (4 - s))
        halves = (1 - way, way) if s == 1 else (way, 1 - way)
        for h in halves:
            if s > 1 or h == way:
                z_copy(way, s - 1, h).wait_recv()
                pb[zd, H[h], :] = pb[zd, H[h], :] + recv1[way, s - 1, H[h], :]
            z_copy(way, s, h).start()

    pass_on(1)
    sol_ref[1] = xg[x, 1]
    keep_x(1)
    product1(4)
    z_copy(0, 0, 0).start()
    z_copy(1, 0, 1).start()
    keep_z()
    product2(1)
    for way in (0, 1):
        x_first(1, way).start()
    feed(9)
    product1(-3)
    product1(3)
    z_step(0, 1)
    z_step(1, 1)
    for way in (0, 1):
        x_first(1, way).wait_recv()
        spot = xpos((1, -1)[way])
        qb[1, spot, H[way], :] = qb[1, spot, H[way], :] + xr0[1, way]
        x_second(1, way).start()
    feed(10)
    product2(0)
    for way in (0, 1):
        x_first(0, way).start()
    product1(-2)
    product1(2)
    z_step(0, 2)
    z_step(1, 2)
    for way in (0, 1):
        x_second(1, way).wait_recv()
    farsum[...] = qb[1, x] + (xr1[1, 0] + xr1[1, 1])
    far_copy = remote(farsum, farrecv, b3_s.at[0], b3_r.at[0], at_z(4))
    far_copy.start()
    for way in (0, 1):
        x_first(0, way).wait_recv()
        spot = xpos((1, -1)[way])
        qb[0, spot, H[way], :] = qb[0, spot, H[way], :] + xr0[0, way]
        x_second(0, way).start()
    product1(-1)
    product1(1)
    z_step(0, 3)
    z_step(1, 3)
    product1(0)
    for p in (0, 1):
        core_copy(p).wait_send()
        cg_copy(p).wait_send()
        for d in (1, 2, 3):
            y_copy(p, d).wait_send()
            gx_copy(p, d).wait_send()
            fx_copy(p, d).wait_send()
        for i in range(4):
            gz_copy(p, i).wait_send()
            fz_copy(p, i).wait_send()
    whole(crecv.at[pl.ds(0, NW - 1)], rs_s.at[0])
    whole(restall.at[pl.ds(0, 8 * (NW - 1))], ag_s.at[0])
    whole(a2.at[:, pl.ds(0, 3)], a2_s.at[0])
    for way in (0, 1):
        x_second(0, way).wait_recv()
    far_copy.wait_recv()
    total2 = qb[0, x] + (xr1[0, 0] + xr1[0, 1]) + farrecv[...]
    out_ref[R1:, :] = loads_ref[R1:, :] - total2.T
    for way in (0, 1):
        for h in (0, 1):
            z_copy(way, 3, h).wait_recv()
    total1 = pb[z] + (recv1[0, 3] + recv1[1, 3])
    out_ref[:R1, :] = loads_ref[:R1, :] - total1.T

    whole(a1.at[pl.ds(0, 6)], a1_s.at[0])
    for far in (0, 1):
        for way in (0, 1):
            x_first(far, way).wait_send()
            x_second(far, way).wait_send()
    z_copy(0, 0, 0).wait_send()
    z_copy(1, 0, 1).wait_send()
    for way in (0, 1):
        for s in (1, 2, 3):
            for h in (0, 1):
                z_copy(way, s, h).wait_send()
    far_copy.wait_send()


def on_device(panel_loads, tail_loads, inverses, cross_factor, tail_factor):
    vmem = pl.BlockSpec(memory_space=pltpu.VMEM)
    dma = pltpu.SemaphoreType.DMA
    scratch = [
        pltpu.VMEM((2, 256, 256), F32),
        pltpu.VMEM((2, 64, 256), F32),
        pltpu.VMEM((64, 256), F32),
        pltpu.VMEM((ROWS, 256), F32),
        pltpu.VMEM((2, 64, 256), F32),
        pltpu.VMEM((2, 32, 256), F32),
        pltpu.VMEM((2, NY, 32, 256), F32),
        pltpu.VMEM((NX, 2, 64, 256), F32),
        pltpu.VMEM((4, 2, 64, 256), F32),
        pltpu.VMEM((256, 256), F32),
        pltpu.VMEM((NW, 8, 256), F32),
        pltpu.VMEM((256, 256), F32),
        pltpu.VMEM((NZ, 2, NX, 64, R1), F32),
        pltpu.VMEM((2, 4, 2, 64, NX * R2), F32),
        pltpu.VMEM((NZ, 256, R1), F32),
        pltpu.VMEM((2, NX, 256, R2), F32),
        pltpu.VMEM((2, 4, 256, R1), F32),
        pltpu.VMEM((2, 2, 128, R2), F32),
        pltpu.VMEM((2, 2, 256, R2), F32),
        pltpu.VMEM((256, R2), F32),
        pltpu.VMEM((256, R2), F32),
        pltpu.VMEM((3, 2, 256, 512), BF16),
        dma((2,)), dma((2,)), dma((2, 4)), dma((2, 4)), dma((2,)), dma((2,)),
        pltpu.SemaphoreType.REGULAR((2,)),
        dma((1,)), dma((1,)), dma((1,)), dma((1,)),
        dma((2, 4)), dma((2, 4)), dma((2, 4)), dma((2, 4)),
        dma((2, 4)), dma((2, 4)), dma((2, 4)), dma((2, 4)),
        dma((1,)), dma((NZ,)), dma((NZ,)),
        dma((1,)), dma((1,)), dma((2, NX)),
        dma((2, 4, 2)), dma((2, 4, 2)), dma((2, 2, 2)), dma((2, 2, 2)), dma((1,)), dma((1,)), dma((4,)),
    ]
    return pl.pallas_call(
        kernel,
        out_shape=(
            jax.ShapeDtypeStruct((2, 64, 256), F32),
            jax.ShapeDtypeStruct((ROWS, 256), F32),
        ),
        in_specs=[pl.BlockSpec(memory_space=pl.ANY)] * 5,
        out_specs=(vmem, vmem),
        scratch_shapes=scratch,
        compiler_params=pltpu.CompilerParams(
            collective_id=0, has_side_effects=True, vmem_limit_bytes=56 * 1024 * 1024
        ),
    )(panel_loads, inverses, cross_factor, tail_loads, tail_factor)


def solution(mesh):
    in_specs = (
        P(None, "narrow", None),
        P(("narrow", "wide"), None),
        P(None, "wide", "narrow"),
        P("wide", "narrow"),
        P(None, "wide", "narrow"),
    )
    out_specs = (P(None, "wide", None), P(("narrow", "wide"), None))
    return jax.shard_map(
        on_device, mesh=mesh, in_specs=in_specs, out_specs=out_specs, check_vma=False
    )
```

```python
import functools

import jax
import jax.numpy as jnp
from jax import lax
from jax.experimental import pallas as pl
from jax.experimental.pallas import tpu as pltpu
from jax.sharding import PartitionSpec as P

MESH = pl.DeviceIdType.MESH
NX, NZ, NY = 4, 8, 4
NW = NX * NZ
ROWS = 384
R1 = 256
R2 = 128
HIGH = lax.Precision.HIGHEST
F32 = jnp.float32
BF16 = jnp.bfloat16
SCHEDULE = {
    0: ((1, 0, 1), (2, 0, 1)),
    1: ((1, 1, 2),),
    2: (),
    3: ((1, 2, 3), (2, 1, 2)),
    4: ((1, 3, 4), (2, 2, 3)),
    6: ((2, 3, 4),),
    7: ((1, 4, 5),),
    8: ((1, 5, 6),),
    9: ((1, 6, 7),),
    10: ((1, 7, 8),),
}


def dot(a, b):
    return jnp.dot(a, b, precision=HIGH, preferred_element_type=F32)


def split(a):
    hi = a.astype(BF16)
    return hi, (a - hi.astype(F32)).astype(BF16)


def dot3(xh, xl, a):
    ah, al = split(a)
    out = jnp.dot(xh, ah, preferred_element_type=F32)
    out += jnp.dot(xl, ah, preferred_element_type=F32)
    return out + jnp.dot(xh, al, preferred_element_type=F32)


def kernel(
    pl_hbm, inv_hbm, cross_hbm, loads_hbm, tail_ref,
    sol_ref, out_ref,
    pl_ref, inv_ref, cross_ref, loads_ref,
    part, corebuf, ybuf, xg, xz, cpart, crecv, restall,
    a1, a2, pb, qb, recv1, xr0, xr1, farsum, farrecv, xt,
    core_s, core_r, y_s, y_r, cg_s, cg_r, known,
    rs_s, rs_r, ag_s, ag_r, gx_s, gx_r, gz_s, gz_r, fx_s, fx_r, fz_s, fz_r,
    a1_s, a1_r, a1_l, a2_s, a2_r, a2_l,
    b1_s, b1_r, b2_s, b2_r, b3_s, b3_r, load,
):
    w = lax.axis_index("wide")
    n = lax.axis_index("narrow")
    x, z = w // NZ, w % NZ
    y, core = n // 2, n % 2

    def xpos(d):
        return (x + d + NX) % NX

    def zpos(d):
        return (z + d + NZ) % NZ

    def at_x(d):
        return (xpos(d) * NZ + z, n)

    def at_z(d):
        return (x * NZ + zpos(d), n)

    def at_y(d):
        return (w, ((y + d) % NY) * 2 + core)

    other = (w, y * 2 + 1 - core)

    def remote(src, dst, ssem, rsem, device):
        return pltpu.make_async_remote_copy(
            src_ref=src, dst_ref=dst, send_sem=ssem, recv_sem=rsem,
            device_id=device, device_id_type=MESH,
        )

    barrier = pltpu.get_barrier_semaphore()
    peers = [at_x(d) for d in (1, 2, 3)] + [at_z(d) for d in (1, -1, 2, -2)]
    peers += [at_y(d) for d in (1, 2, 3)] + [other]
    for device in peers:
        pl.semaphore_signal(barrier, inc=1, device_id=device, device_id_type=MESH)

    loads = [
        pltpu.make_async_copy(src, dst, load.at[i])
        for i, (src, dst) in enumerate((
            (pl_hbm, pl_ref), (inv_hbm, inv_ref), (cross_hbm, cross_ref), (loads_hbm, loads_ref),
        ))
    ]
    for copy in loads:
        copy.start()

    def lanes1(xd, zd):
        return pl.ds(pl.multiple_of((xd * NZ + zd) * ROWS, 128), R1)

    def lanes2(xd, zd):
        return pl.ds(pl.multiple_of((xd * NZ + zd) * ROWS + R1, 128), R2)

    def own1(zd):
        return pltpu.make_async_copy(
            tail_ref.at[:, :, lanes1(x, zd)], a1.at[zd, :, x], a1_l.at[zd]
        )

    def own2(xd, far):
        zd = zpos(4 * far)
        return pltpu.make_async_copy(
            tail_ref.at[:, :, lanes2(xd, zd)],
            a2.at[far, 0, :, :, pl.ds(pl.multiple_of(xd * R2, R2), R2)], a2_l.at[far, xd],
        )

    def send1(d, zd):
        return remote(
            tail_ref.at[:, :, lanes1(xpos(d), zd)], a1.at[zd, :, x],
            a1_s.at[0], a1_r.at[zd], at_x(d),
        )

    def send2(i, xd, far):
        d = (1, -1, 2, -2)[i]
        zd = zpos(d + 4 * far)
        to = pl.ds(pl.multiple_of(xd * R2, R2), R2)
        if i < 2:
            src = tail_ref.at[:, :, lanes2(xd, zd)]
            dst = a2.at[far, 1 + i, :, :, to]
        else:
            src = tail_ref.at[far, :, lanes2(xd, zd)]
            dst = a2.at[far, 3, i - 2, :, to]
        return remote(src, dst, a2_s.at[0], a2_r.at[0], at_z(d))

    def feed1(first, last):
        def body(i, carry):
            zd = zpos((4 - (i + 1) // 2) * (1 - 2 * (i % 2)))
            for d in (2, 1, 3):
                send1(d, zd).start()
            own1(zd).start()
            return carry
        lax.fori_loop(first, last, body, 0)

    def feed2(first, last):
        def body(xd, carry):
            for far in (1, 0):
                for i in (2, 3, 0, 1):
                    send2(i, xd, far).start()
                own2(xd, far).start()
            return carry
        lax.fori_loop(first, last, body, 0)

    def feed(stage):
        for kind, first, last in SCHEDULE[stage]:
            (feed1 if kind == 1 else feed2)(first, last)

    def whole(like, sem):
        pltpu.make_async_copy(like, like, sem).wait()

    for copy in loads:
        copy.wait()
    crossT = cross_ref[...].T
    part[0] = dot(inv_ref[0], pl_ref[0])

    pl.semaphore_wait(barrier, len(peers))
    for d in (1, 2, 3):
        pl.semaphore_signal(known.at[0], inc=1, device_id=at_x(d), device_id_type=MESH)

    half = 32
    mine = pl.ds(pl.multiple_of(core * half, half), half)
    theirs = pl.ds(pl.multiple_of((1 - core) * half, half), half)

    def core_copy(p):
        return remote(part.at[p, theirs], corebuf.at[p], core_s.at[p], core_r.at[p], other)

    def y_copy(p, d):
        return remote(
            ybuf.at[p, y], ybuf.at[p, y], y_s.at[p, d], y_r.at[p, 4 - d], at_y(d)
        )

    def cg_copy(p):
        return remote(
            xg.at[x, p, mine], xg.at[x, p, mine], cg_s.at[p], cg_r.at[p], other
        )

    def gx_copy(p, d):
        return remote(
            xg.at[x, p, mine], xg.at[x, p, mine], gx_s.at[p, d], gx_r.at[p, 4 - d], at_x(d)
        )

    def gz_copy(p, i):
        d = (1, -1, 2, -2)[i]
        return remote(
            xg.at[x, p, mine], xz.at[i, p, mine], gz_s.at[p, i], gz_r.at[p, i], at_z(d)
        )

    def fx_copy(p, d):
        return remote(
            xg.at[xpos(d), p, mine], xg.at[xpos(d), p, mine],
            fx_s.at[p, d], fx_r.at[p, d], other,
        )

    def fz_copy(p, i):
        return remote(
            xz.at[i, p, mine], xz.at[i, p, mine], fz_s.at[p, i], fz_r.at[p, i], other
        )

    def pass_on(p):
        for d in (1, 3, 2):
            gx_copy(p, 4 - d).wait_recv()
            fx_copy(p, d).start()
        for i in range(4):
            gz_copy(p, i).wait_recv()
            fz_copy(p, i).start()

    def sum_narrow(p):
        core_copy(p).start()
        feed(6 * p)
        core_copy(p).wait_recv()
        ybuf[p, y] = part[p, mine] + corebuf[p]
        for d in (2, 1, 3):
            y_copy(p, d).start()
        if p == 0:
            pl.semaphore_wait(known.at[0], 3)
            for d in (2, -2):
                pl.semaphore_signal(
                    known.at[1], inc=1, device_id=at_z(d), device_id_type=MESH
                )
        feed(6 * p + 1)
        for d in (2, 1, 3):
            y_copy(p, d).wait_recv()
        xg[x, p, mine] = (ybuf[p, 0] + ybuf[p, 1]) + (ybuf[p, 2] + ybuf[p, 3])
        cg_copy(p).start()
        for d in (2, 1, 3):
            gx_copy(p, d).start()
        for i in (2, 3, 0, 1):
            gz_copy(p, i).start()
        feed(6 * p + 2)
        cg_copy(p).wait_recv()

    sum_narrow(0)

    def keep(which, spot, value):
        hi, lo = split(value.T)
        xt[which, 0, :, spot] = hi
        xt[which, 1, :, spot] = lo

    def keep_x(p):
        for d in (1, 2, 3):
            fx_copy(p, d).wait_recv()
        keep(0, pl.ds(p * 256, 256), xg[:, p].reshape(256, 256))

    cpart[...] = dot(crossT, xg[x, 0])
    pl.semaphore_wait(known.at[1], 2)

    def rows_of(i):
        return pl.ds(pl.multiple_of(i * 8, 8), 8)

    def peer(j):
        dz = (4 - (j // 4 + 1) // 2) * (1 - 2 * (j // 4 % 2))
        q = j % 4
        dx = 2 + (q + 1) // 2 * (1 - 2 * (q % 2))
        return xpos(dx) * NZ + zpos(dz)

    def rs_copy(j):
        to = peer(j)
        return remote(cpart.at[rows_of(to)], crecv.at[w], rs_s.at[0], rs_r.at[0], (to, n))

    def ag_copy(j):
        return remote(
            restall.at[rows_of(w)], restall.at[rows_of(w)], ag_s.at[0], ag_r.at[0], (peer(j), n)
        )

    def to_peers(copy):
        def body(j, carry):
            copy(j).start()
            return carry
        lax.fori_loop(0, NW - 1, body, 0)

    to_peers(rs_copy)
    feed(3)
    crecv[w] = cpart[rows_of(w), :]
    whole(crecv.at[pl.ds(0, NW - 1)], rs_r.at[0])
    restall[rows_of(w), :] = pl_ref[1, rows_of(w), :] - jnp.sum(crecv[...], axis=0)
    to_peers(ag_copy)
    feed(4)
    pass_on(0)
    sol_ref[0] = xg[x, 0]
    keep_x(0)
    whole(restall.at[pl.ds(0, 8 * (NW - 1))], ag_r.at[0])

    part[1] = dot(inv_ref[1], restall[...])
    sum_narrow(1)

    def keep_z():
        for p in (0, 1):
            for i in range(4):
                fz_copy(p, i).wait_recv()
        around = [xg[x].reshape(128, 256), xz[0].reshape(128, 256), xz[1].reshape(128, 256)]
        keep(1, pl.ds(0, 512), jnp.concatenate(around + [xz[2, 0], xz[3, 0]], axis=0))
        keep(2, pl.ds(0, 512), jnp.concatenate(around + [xz[2, 1], xz[3, 1]], axis=0))
        whole(a2.at[:, pl.ds(0, 3)], a2_r.at[0])
        for far in (0, 1):
            for xd in range(NX):
                own2(xd, far).wait()

    def product2(far):
        value = dot3(xt[1 + far, 0], xt[1 + far, 1], a2[far].reshape(512, NX * R2))
        for xd in range(NX):
            qb[far, xd] = value[:, xd * R2:(xd + 1) * R2]

    H = (pl.ds(0, 128), pl.ds(128, 128))

    def x_first(far, way):
        return remote(
            qb.at[far, xpos(2), H[way]], xr0.at[far, way],
            b2_s.at[far, way, 0], b2_r.at[far, way, 0], at_x((1, -1)[way]),
        )

    def x_second(far, way):
        d = (1, -1)[way]
        return remote(
            qb.at[far, xpos(d)], xr1.at[far, way],
            b2_s.at[far, way, 1], b2_r.at[far, way, 1], at_x(d),
        )

    def z_copy(way, s, h):
        d = (-1, 1)[way]
        return remote(
            pb.at[zpos(d * (4 - s)), H[h]], recv1.at[way, s, H[h]],
            b1_s.at[way, s, h], b1_r.at[way, s, h], at_z(d),
        )

    def product1(d):
        zd = zpos(d)
        own1(zd).wait()
        whole(a1.at[zd, :, pl.ds(0, NX - 1)], a1_r.at[zd])
        pb[zd] = dot3(xt[0, 0], xt[0, 1], a1[zd].reshape(512, R1))

    def z_step(way, s):
        zd = zpos((-1, 1)[way] * (4 - s))
        halves = (1 - way, way) if s == 1 else (way, 1 - way)
        for h in halves:
            if s > 1 or h == way:
                z_copy(way, s - 1, h).wait_recv()
                pb[zd, H[h], :] = pb[zd, H[h], :] + recv1[way, s - 1, H[h], :]
            z_copy(way, s, h).start()

    pass_on(1)
    sol_ref[1] = xg[x, 1]
    keep_x(1)
    product1(4)
    z_copy(0, 0, 0).start()
    z_copy(1, 0, 1).start()
    keep_z()
    product2(1)
    for way in (0, 1):
        x_first(1, way).start()
    product1(-3)
    product1(3)
    feed(9)
    z_step(0, 1)
    z_step(1, 1)
    for way in (0, 1):
        x_first(1, way).wait_recv()
        spot = xpos((1, -1)[way])
        qb[1, spot, H[way], :] = qb[1, spot, H[way], :] + xr0[1, way]
        x_second(1, way).start()
    feed(10)
    product2(0)
    for way in (0, 1):
        x_first(0, way).start()
    product1(-2)
    product1(2)
    z_step(0, 2)
    z_step(1, 2)
    for way in (0, 1):
        x_second(1, way).wait_recv()
    farsum[...] = qb[1, x] + (xr1[1, 0] + xr1[1, 1])
    far_copy = remote(farsum, farrecv, b3_s.at[0], b3_r.at[0], at_z(4))
    far_copy.start()
    for way in (0, 1):
        x_first(0, way).wait_recv()
        spot = xpos((1, -1)[way])
        qb[0, spot, H[way], :] = qb[0, spot, H[way], :] + xr0[0, way]
        x_second(0, way).start()
    product1(-1)
    product1(1)
    z_step(0, 3)
    z_step(1, 3)
    product1(0)
    for p in (0, 1):
        core_copy(p).wait_send()
        cg_copy(p).wait_send()
        for d in (1, 2, 3):
            y_copy(p, d).wait_send()
            gx_copy(p, d).wait_send()
            fx_copy(p, d).wait_send()
        for i in range(4):
            gz_copy(p, i).wait_send()
            fz_copy(p, i).wait_send()
    whole(crecv.at[pl.ds(0, NW - 1)], rs_s.at[0])
    whole(restall.at[pl.ds(0, 8 * (NW - 1))], ag_s.at[0])
    whole(a2.at[:, pl.ds(0, 3)], a2_s.at[0])
    for way in (0, 1):
        x_second(0, way).wait_recv()
    far_copy.wait_recv()
    total2 = qb[0, x] + (xr1[0, 0] + xr1[0, 1]) + farrecv[...]
    out_ref[R1:, :] = loads_ref[R1:, :] - total2.T
    for way in (0, 1):
        for h in (0, 1):
            z_copy(way, 3, h).wait_recv()
    total1 = pb[z] + (recv1[0, 3] + recv1[1, 3])
    out_ref[:R1, :] = loads_ref[:R1, :] - total1.T

    whole(a1.at[pl.ds(0, 6)], a1_s.at[0])
    for far in (0, 1):
        for way in (0, 1):
            x_first(far, way).wait_send()
            x_second(far, way).wait_send()
    z_copy(0, 0, 0).wait_send()
    z_copy(1, 0, 1).wait_send()
    for way in (0, 1):
        for s in (1, 2, 3):
            for h in (0, 1):
                z_copy(way, s, h).wait_send()
    far_copy.wait_send()


def on_device(panel_loads, tail_loads, inverses, cross_factor, tail_factor):
    vmem = pl.BlockSpec(memory_space=pltpu.VMEM)
    dma = pltpu.SemaphoreType.DMA
    scratch = [
        pltpu.VMEM((2, 256, 256), F32),
        pltpu.VMEM((2, 64, 256), F32),
        pltpu.VMEM((64, 256), F32),
        pltpu.VMEM((ROWS, 256), F32),
        pltpu.VMEM((2, 64, 256), F32),
        pltpu.VMEM((2, 32, 256), F32),
        pltpu.VMEM((2, NY, 32, 256), F32),
        pltpu.VMEM((NX, 2, 64, 256), F32),
        pltpu.VMEM((4, 2, 64, 256), F32),
        pltpu.VMEM((256, 256), F32),
        pltpu.VMEM((NW, 8, 256), F32),
        pltpu.VMEM((256, 256), F32),
        pltpu.VMEM((NZ, 2, NX, 64, R1), F32),
        pltpu.VMEM((2, 4, 2, 64, NX * R2), F32),
        pltpu.VMEM((NZ, 256, R1), F32),
        pltpu.VMEM((2, NX, 256, R2), F32),
        pltpu.VMEM((2, 4, 256, R1), F32),
        pltpu.VMEM((2, 2, 128, R2), F32),
        pltpu.VMEM((2, 2, 256, R2), F32),
        pltpu.VMEM((256, R2), F32),
        pltpu.VMEM((256, R2), F32),
        pltpu.VMEM((3, 2, 256, 512), BF16),
        dma((2,)), dma((2,)), dma((2, 4)), dma((2, 4)), dma((2,)), dma((2,)),
        pltpu.SemaphoreType.REGULAR((2,)),
        dma((1,)), dma((1,)), dma((1,)), dma((1,)),
        dma((2, 4)), dma((2, 4)), dma((2, 4)), dma((2, 4)),
        dma((2, 4)), dma((2, 4)), dma((2, 4)), dma((2, 4)),
        dma((1,)), dma((NZ,)), dma((NZ,)),
        dma((1,)), dma((1,)), dma((2, NX)),
        dma((2, 4, 2)), dma((2, 4, 2)), dma((2, 2, 2)), dma((2, 2, 2)), dma((1,)), dma((1,)), dma((4,)),
    ]
    return pl.pallas_call(
        kernel,
        out_shape=(
            jax.ShapeDtypeStruct((2, 64, 256), F32),
            jax.ShapeDtypeStruct((ROWS, 256), F32),
        ),
        in_specs=[pl.BlockSpec(memory_space=pl.ANY)] * 5,
        out_specs=(vmem, vmem),
        scratch_shapes=scratch,
        compiler_params=pltpu.CompilerParams(
            collective_id=0, has_side_effects=True, vmem_limit_bytes=56 * 1024 * 1024
        ),
    )(panel_loads, inverses, cross_factor, tail_loads, tail_factor)


def solution(mesh):
    in_specs = (
        P(None, "narrow", None),
        P(("narrow", "wide"), None),
        P(None, "wide", "narrow"),
        P("wide", "narrow"),
        P(None, "wide", "narrow"),
    )
    out_specs = (P(None, "wide", None), P(("narrow", "wide"), None))
    return jax.shard_map(
        on_device, mesh=mesh, in_specs=in_specs, out_specs=out_specs, check_vma=False
    )
```
